32 devices in a mesh: shot: 2 (over x), freq: 8 (over z, y), tile: 2 (over core).
Axes of the slice: x: 2, y: 2, z: 4, core: 2. Of those that a mesh axis runs over, the one named last changes fastest.
Arguments:
- source_field: float32 [4, 8, 64, 1024], P('shot', 'freq', 'tile'), parts along dimension 0, may hold values from -6 to 6
- receiver_field: float32 [4, 8, 64, 1024], P('shot', 'freq', 'tile'), parts along dimension 0, may hold values from -6 to 6
- slowness: float32 [3, 64, 1024], P(None, 'tile', 'freq'), may hold values from 0.5 to 2
- omegas: float32 [8], P('freq'), may hold values from 1.5 to 5
Outputs:
- image_steps: float32 [6, 64, 1024], P('shot', 'tile'), parts along dimension 0
- illumination: float32 [6, 64, 1024], P('shot', 'tile'), parts along dimension 0
The draws below stay inside these ranges and needn't reach their ends.
There are 2 independent parts, one for each index of `shot`. The reference program is written for one: setup_inputs(seed, part) draws one part's arguments, and reference() takes and returns one part's arrays. A program takes and returns all parts, laid end to end along the dimension named above; an argument that names none is the same for every part. Nothing has to cross between parts.
All inputs are finite; a program needn't handle non-finite values.
Results may differ from the reference program's by a relative error of at most 0.0003.
Values sent between devices are 32-bit elements; how exact they have to be, the bound alone decides.
No kernel may reach another device: no remote copies, remote signals or barrier semaphores. Data moves between devices by JAX's collectives and lax.ppermute only.
A program may use at most 64 MiB of HBM per device.

```python
import math
import jax
import jax.numpy as jnp
from jax import lax

NY = 1024
STEPS = 3
TERMS = 10
NODES = 16
NF = 8
NX = 64


def block_levels(rng, dims, shards, least, high):
    gain = 1.0
    for axis_at, shards_of in shards:
        steps = jax.random.uniform(jax.random.fold_in(jax.random.fold_in(rng, 6), axis_at), (shards_of,), jnp.float32, least / len(shards), high / len(shards))
        gain = gain * jnp.repeat(jnp.exp(steps), dims[axis_at] // shards_of).reshape((-1,) + (1,) * (len(dims) - 1 - axis_at))
    return gain


def centred(key, extent, width, most, split=(), held_as=jnp.bfloat16):
    level = block_levels(key, extent, split, -0.22, 0.18) if split else 1.0
    array = jax.random.normal(key, extent, jnp.float32) * width * level
    return jnp.minimum(jnp.maximum(array, -most), most).astype(held_as)


def setup_inputs(seed: int = 0, part: int = 0) -> dict:
    keys = jax.random.split(jax.random.key(seed), 5)
    own_keys = jax.random.split(jax.random.fold_in(keys[4], part), 5)
    return {
        "source_field": centred(own_keys[0], (2, NF, NX, NY), 1.0, 6.0, ((1, 8), (2, 2)), jnp.float32),
        "receiver_field": centred(own_keys[1], (2, NF, NX, NY), 1.0, 6.0, ((1, 8), (2, 2)), jnp.float32),
        "slowness": jnp.clip(0.5 + 1.5 * jax.random.uniform(keys[2], (STEPS, NX, NY), jnp.float32) ** block_levels(keys[2], (STEPS, NX, NY), ((1, 2), (2, 8)), -0.2, 0.2), 0.5, 2.0),
        "omegas": jnp.clip(jnp.exp(math.log(5.0) - 1.2039728 * jax.random.uniform(keys[3], (NF,), jnp.float32) ** block_levels(keys[3], (NF,), ((0, 8),), -0.2, 0.2)), 1.5, 5.0),
    }


def mcclellan_rows(padded):
    along_x = 0.5 * padded[:, :, :-2] + padded[:, :, 1:-1] + 0.5 * padded[:, :, 2:]
    widened = jnp.pad(along_x, ((0, 0), (0, 0), (0, 0), (1, 1)))
    along_y = 0.5 * widened[..., :-2] + widened[..., 1:-1] + 0.5 * widened[..., 2:]
    return 0.5 * along_y - padded[:, :, 1:-1]

def mcclellan_full(fields):
    return mcclellan_rows(jnp.pad(fields, ((0, 0), (0, 0), (1, 1), (0, 0))))

def coefficients(omega_values, slow_slab):
    node_angles = (jnp.arange(NODES, dtype=jnp.float32) + 0.5) * (math.pi / NODES)
    orders = jnp.arange(TERMS, dtype=jnp.float32)
    weights = jnp.where(orders == 0, 1.0, 2.0) / NODES
    cheb_table = jnp.cos(node_angles[:, None] * orders[None, :]) * weights[None, :]
    phase_arg = omega_values[:, None, None, None] * jnp.cos(node_angles)[None, :, None, None] * slow_slab[None, None]
    coef_real = jnp.einsum('fmxy,mn->fnxy', jnp.cos(phase_arg), cheb_table, precision=lax.Precision.HIGHEST)
    coef_imag = jnp.einsum('fmxy,mn->fnxy', jnp.sin(phase_arg), cheb_table, precision=lax.Precision.HIGHEST)
    return (coef_real, coef_imag)

def apply_terms(summed, coef_real, coef_imag, cheb_term):
    source_real, source_imag, receiver_real, receiver_imag = (cheb_term[0], cheb_term[1], cheb_term[2], cheb_term[3])
    return summed + jnp.stack([coef_real * source_real - coef_imag * source_imag, coef_real * source_imag + coef_imag * source_real, coef_real * receiver_real + coef_imag * receiver_imag, coef_real * receiver_imag - coef_imag * receiver_real])

def extrapolate(fields, coef_real, coef_imag):
    prev_term = fields
    this_term = mcclellan_full(fields)
    summed = apply_terms(jnp.zeros_like(fields), coef_real[:, 0], coef_imag[:, 0], prev_term)
    summed = apply_terms(summed, coef_real[:, 1], coef_imag[:, 1], this_term)
    for term_order in range(2, TERMS):
        next_term = 2.0 * mcclellan_full(this_term) - prev_term
        summed = apply_terms(summed, coef_real[:, term_order], coef_imag[:, term_order], next_term)
        prev_term, this_term = (this_term, next_term)
    return summed

def reference(source_field, receiver_field, slowness, omegas):
    fields = jnp.concatenate([source_field, receiver_field], 0)
    image_list = []
    energy_list = []
    for depth_index in range(STEPS):
        coef_real, coef_imag = coefficients(omegas, slowness[depth_index])
        fields = extrapolate(fields, coef_real, coef_imag)
        image_list.append(lax.optimization_barrier(jnp.sum(fields[0] * fields[2] + fields[1] * fields[3], axis=0)) / math.sqrt(NF))
        energy_list.append(lax.optimization_barrier(jnp.sum(fields[0] * fields[0] + fields[1] * fields[1], axis=0)) / NF)
    return (jnp.stack(image_list), jnp.stack(energy_list))
```

```python
import math

import jax
import jax.numpy as jnp
from jax import lax
from jax.experimental import pallas as pl
from jax.experimental.pallas import tpu as pltpu
from jax.sharding import PartitionSpec as P

STEPS = 3
TERMS = 10
NODES = 16
MARGIN = TERMS - 1
LANES = 128
ROWS = 8

LARGEST = 10.02
DEGREE = 11


def node_sum(order, product):
    wave = math.cos if order % 2 == 0 else math.sin
    weight = (1.0 if order == 0 else 2.0) / NODES
    angles = [math.pi * (m + 0.5) / NODES for m in range(NODES)]
    return weight * math.fsum(wave(product * math.cos(t)) * math.cos(order * t) for t in angles)


def polynomial(order):
    count = 64
    angles = [math.pi * (k + 0.5) / count for k in range(count)]
    samples = []
    for angle in angles:
        product = LARGEST * math.sqrt(0.5 * (math.cos(angle) + 1.0))
        value = node_sum(order, product)
        samples.append(value if order % 2 == 0 else value / product)
    cheb = [
        (1.0 if n == 0 else 2.0) / count * math.fsum(s * math.cos(n * t) for s, t in zip(samples, angles))
        for n in range(DEGREE + 1)
    ]
    powers = [0.0] * (DEGREE + 1)
    before, here = [1.0], [0.0, 1.0]
    for n in range(DEGREE + 1):
        now = before if n == 0 else here
        for k, c in enumerate(now):
            powers[k] += cheb[n] * c
        if n >= 1:
            after = [0.0] + [2.0 * c for c in here]
            for k, c in enumerate(before):
                after[k] -= c
            before, here = here, after
    return powers


POLYNOMIALS = [polynomial(n) for n in range(TERMS)]


def blocks_for(rows, most):
    return min(most, -(-rows // ROWS))


def depth_kernel(depth, tile_rows, width, scales, *refs):
    first, last = depth == 0, depth == STEPS - 1
    refs = list(refs)
    omega_ref = refs.pop(0)
    if first:
        own_fields, other_fields = (refs.pop(0), refs.pop(0)), (refs.pop(0), refs.pop(0))
    else:
        fields_ref = refs.pop(0)
    own_slow, other_slow = refs.pop(0), refs.pop(0)
    if not last:
        next_ref = refs.pop(0)
    maps_ref = refs.pop(0)
    terms_ref, coef_ref = refs.pop(0), refs.pop(0)
    if last:
        next_ref = refs.pop(0)

    own = tile_rows // ROWS
    total = 2 * own
    columns = width // LANES
    out_rows = tile_rows + MARGIN * (STEPS - 1 - depth)
    out_blocks = blocks_for(out_rows, total)
    in_blocks = blocks_for(out_rows + MARGIN, total)
    tile = lax.axis_index("tile")
    lane = lax.broadcasted_iota(jnp.int32, (ROWS, LANES), 1)
    row = lax.broadcasted_iota(jnp.int32, (ROWS, LANES), 0)
    lane_first, lane_last = lane == 0, lane == LANES - 1
    row_first, row_last = row == 0, row == ROWS - 1
    zero = jnp.zeros((ROWS, LANES), jnp.float32)

    def place(b):
        return jnp.where(tile == 0, b, total - 1 - b)

    def own_place(b):
        return jnp.where(tile == 0, b, own - 1 - b)

    def other_place(b):
        return jnp.where(tile == 0, b - own, total - 1 - b)

    def cols(j):
        return slice(j * LANES, (j + 1) * LANES)

    def rows_at(block):
        return pl.ds(pl.multiple_of(block * ROWS, ROWS), ROWS)

    for slot in range(3):
        for c in range(4):
            for edge in (0, total + 1):
                for j in range(columns):
                    terms_ref[slot, c, edge, :, cols(j)] = zero
    if first:
        for b in range(total):
            sources = own_fields if b < own else other_fields
            at = own_place(b) if b < own else other_place(b)
            for c in range(4):
                terms_ref[0, c, place(b) + 1] = sources[c // 2][c % 2, 0, rows_at(at), :]
    else:
        for b in range(in_blocks):
            for c in range(4):
                terms_ref[0, c, place(b) + 1] = fields_ref[c, place(b)]
    for slot in range(3):
        if in_blocks < total:
            for c in range(4):
                for j in range(columns):
                    terms_ref[slot, c, place(in_blocks) + 1, :, cols(j)] = zero

    omega = omega_ref[0]

    def coefficients(b, slow_ref, at):
        for j in range(columns):
            product = slow_ref[j, depth, rows_at(at), :] * omega
            u = product * product * (2.0 / LARGEST**2) - 1.0
            for n in range(TERMS):
                value = u * POLYNOMIALS[n][DEGREE] + POLYNOMIALS[n][DEGREE - 1]
                for k in range(DEGREE - 2, -1, -1):
                    value = value * u + POLYNOMIALS[n][k]
                if n % 2 == 1:
                    value = value * product
                coef_ref[n, b, :, cols(j)] = value

    def own_coefficients(b, carry):
        coefficients(b, own_slow, own_place(b))
        return carry

    def other_coefficients(b, carry):
        coefficients(b, other_slow, other_place(b))
        return carry

    lax.fori_loop(0, own, own_coefficients, 0)
    if out_blocks > own:
        lax.fori_loop(own, out_blocks, other_coefficients, 0)

    def stencil(slot, c, at):
        centre, summed = [], []
        for j in range(columns):
            p = terms_ref[slot, c, at + 1, :, cols(j)]
            above = terms_ref[slot, c, at, :, cols(j)]
            below = terms_ref[slot, c, at + 2, :, cols(j)]
            up = jnp.where(row_first, pltpu.roll(above, 1, 0), pltpu.roll(p, 1, 0))
            down = jnp.where(row_last, pltpu.roll(below, ROWS - 1, 0), pltpu.roll(p, ROWS - 1, 0))
            centre.append(p)
            summed.append((p + p) + (up + down))
        left = [pltpu.roll(x, 1, 1) for x in summed]
        right = [pltpu.roll(x, LANES - 1, 1) for x in summed]
        result = []
        for j in range(columns):
            low = jnp.where(lane_first, left[j - 1] if j else zero, left[j])
            high = jnp.where(lane_last, right[j + 1] if j + 1 < columns else zero, right[j])
            x = summed[j]
            result.append((x + x) + (low + high))
        return centre, result

    def next_term(n, c, at):
        centre, wide = stencil((n - 1) % 3, c, at)
        result = []
        for j in range(columns):
            if n == 1:
                value = 0.125 * wide[j] - centre[j]
            else:
                before = terms_ref[(n - 2) % 3, c, at + 1, :, cols(j)]
                value = 0.25 * wide[j] - (centre[j] + centre[j]) - before
            result.append(value)
            if n < TERMS - 1:
                terms_ref[n % 3, c, at + 1, :, cols(j)] = value
        return centre, result

    def accumulate(n, b, imaging):
        at = place(b)
        both = [next_term(n, c, at) for c in range(4)]
        for j in range(columns):
            h = coef_ref[n, b, :, cols(j)]
            t = [both[c][1][j] for c in range(4)]
            if n == 1:
                h0 = coef_ref[0, b, :, cols(j)]
                total_here = [h0 * both[c][0][j] for c in range(4)]
            else:
                total_here = [next_ref[c, at, :, cols(j)] for c in range(4)]
            if n % 2 == 0:
                total_here = [s + h * x for s, x in zip(total_here, t)]
            else:
                total_here = [
                    total_here[0] - h * t[1],
                    total_here[1] + h * t[0],
                    total_here[2] + h * t[3],
                    total_here[3] - h * t[2],
                ]
            if not (last and n == TERMS - 1):
                for c in range(4):
                    next_ref[c, at, :, cols(j)] = total_here[c]
            if imaging:
                s_re, s_im, r_re, r_im = total_here
                at_own = own_place(b)
                maps_ref[rows_at(at_own), cols(j)] = (s_re * r_re + s_im * r_im) * scales[0]
                maps_ref[rows_at(own + at_own), cols(j)] = (s_re * s_re + s_im * s_im) * scales[1]

    for n in range(1, TERMS):
        needed = blocks_for(out_rows + MARGIN - n, total)
        if n < TERMS - 1:
            lax.fori_loop(0, out_blocks, lambda b, carry, n=n: accumulate(n, b, False), None)
            for b in range(out_blocks, needed):
                for c in range(4):
                    next_term(n, c, place(b))
        else:
            lax.fori_loop(0, own, lambda b, carry, n=n: accumulate(n, b, True), None)
            if out_blocks > own:
                lax.fori_loop(own, out_blocks, lambda b, carry, n=n: accumulate(n, b, False), None)


def migrate(depth, omegas, fields, slow, other_slow, tile_rows, width, scales):
    total = 2 * tile_rows // ROWS
    out_rows = tile_rows + MARGIN * (STEPS - 1 - depth)
    out_blocks = blocks_for(out_rows, total)
    last = depth == STEPS - 1
    maps = jax.ShapeDtypeStruct((2 * tile_rows, width), jnp.float32)
    state = (4, total, ROWS, width)
    vmem = pl.BlockSpec(memory_space=pltpu.VMEM)
    scratch = [
        pltpu.VMEM((3, 4, total + 2, ROWS, width), jnp.float32),
        pltpu.VMEM((TERMS, out_blocks, ROWS, width), jnp.float32),
    ]
    if last:
        out_shape, out_specs = (maps,), (vmem,)
        scratch.append(pltpu.VMEM(state, jnp.float32))
    else:
        out_shape, out_specs = (jax.ShapeDtypeStruct(state, jnp.float32), maps), (vmem, vmem)

    def body(*refs):
        depth_kernel(depth, tile_rows, width, scales, *refs)

    vregs = 4 * 9 * out_blocks * (width // LANES)
    return pl.pallas_call(
        body,
        out_shape=out_shape,
        in_specs=[pl.BlockSpec(memory_space=pltpu.SMEM)] + [vmem] * (len(fields) + 2),
        out_specs=out_specs,
        scratch_shapes=scratch,
        compiler_params=pltpu.CompilerParams(vmem_limit_bytes=40 * 2**20),
        cost_estimate=pl.CostEstimate(flops=vregs * 16 * 1024, bytes_accessed=2 * 2**20, transcendentals=0),
        name="migrate",
    )(omegas, *fields, slow, other_slow)


def gather(shard, axis):
    count = lax.axis_size(axis)
    return lax.all_to_all(jnp.broadcast_to(shard[None], (count,) + shard.shape), axis, 0, 0)


def per_device(source_field, receiver_field, slowness, omegas):
    tiles = lax.axis_size("tile")
    assert tiles == 2
    swap = [(0, 1), (1, 0)]
    freqs = lax.axis_size("freq")
    tile_rows, width = source_field.shape[2], source_field.shape[3]
    image_scale = 1.0 / math.sqrt(omegas.shape[0] * freqs)
    energy_scale = 1.0 / (omegas.shape[0] * freqs)

    other_source = lax.ppermute(source_field, "tile", swap)
    other_receiver = lax.ppermute(receiver_field, "tile", swap)
    slow = gather(slowness, "freq")
    if slow.shape[-1] != LANES:
        slow = jnp.moveaxis(slow, 0, 2).reshape(STEPS, tile_rows, width // LANES, LANES)
        slow = jnp.moveaxis(slow, 2, 0)
    other_slow = lax.ppermute(slow, "tile", swap)

    fields = (source_field, receiver_field, other_source, other_receiver)
    images, energies = [], []
    for depth in range(STEPS):
        out = migrate(
            depth, omegas, fields, slow, other_slow, tile_rows, width, (image_scale, energy_scale)
        )
        fields, maps = out[:-1], out[-1]
        parts = lax.all_to_all(
            maps.reshape((freqs, 2 * tile_rows // freqs, width)), "freq", 0, 0
        )
        summed = gather(jnp.sum(parts, axis=0), "freq").reshape(2 * tile_rows, width)
        images.append(summed[:tile_rows])
        energies.append(summed[tile_rows:])
    return (jnp.stack(images), jnp.stack(energies))


def solution(mesh):
    in_specs = (
        P("shot", "freq", "tile", None),
        P("shot", "freq", "tile", None),
        P(None, "tile", "freq"),
        P("freq"),
    )
    out_specs = (P("shot", "tile", None), P("shot", "tile", None))
    return jax.shard_map(
        per_device, mesh=mesh, in_specs=in_specs, out_specs=out_specs, check_vma=False
    )
```

```python
import math

import jax
import jax.numpy as jnp
from jax import lax
from jax.experimental import pallas as pl
from jax.experimental.pallas import tpu as pltpu
from jax.sharding import PartitionSpec as P

STEPS = 3
TERMS = 10
NODES = 16
MARGIN = TERMS - 1
LANES = 128
ROWS = 8

LARGEST = 10.02
DEGREE = 11


def node_sum(order, product):
    wave = math.cos if order % 2 == 0 else math.sin
    weight = (1.0 if order == 0 else 2.0) / NODES
    angles = [math.pi * (m + 0.5) / NODES for m in range(NODES)]
    return weight * math.fsum(wave(product * math.cos(t)) * math.cos(order * t) for t in angles)


def polynomial(order):
    count = 64
    angles = [math.pi * (k + 0.5) / count for k in range(count)]
    samples = []
    for angle in angles:
        product = LARGEST * math.sqrt(0.5 * (math.cos(angle) + 1.0))
        value = node_sum(order, product)
        samples.append(value if order % 2 == 0 else value / product)
    cheb = [
        (1.0 if n == 0 else 2.0) / count * math.fsum(s * math.cos(n * t) for s, t in zip(samples, angles))
        for n in range(DEGREE + 1)
    ]
    powers = [0.0] * (DEGREE + 1)
    before, here = [1.0], [0.0, 1.0]
    for n in range(DEGREE + 1):
        now = before if n == 0 else here
        for k, c in enumerate(now):
            powers[k] += cheb[n] * c
        if n >= 1:
            after = [0.0] + [2.0 * c for c in here]
            for k, c in enumerate(before):
                after[k] -= c
            before, here = here, after
    return powers


ROOTS = (0.0, 0.95, 0.4, 0.75)


def basis_change():
    half = TERMS // 2

    def times(poly, factor):
        out = [0.0] * (len(poly) + len(factor) - 1)
        for i, a in enumerate(poly):
            for j, b in enumerate(factor):
                out[i + j] += a * b
        return out

    basis = [[1.0]]
    for n in range(1, TERMS):
        if n % 2 == 1:
            basis.append(times(basis[-1], [0.0, 8.0]))
        else:
            basis.append(times(basis[n - 2], [-64.0 * ROOTS[n // 2 - 1], 0.0, 64.0]))
    cheb = [[1.0], [0.0, 1.0]]
    for n in range(2, TERMS):
        new = [0.0] + [2.0 * c for c in cheb[-1]]
        for k, c in enumerate(cheb[n - 2]):
            new[k] -= c
        cheb.append(new)
    change = [[0.0] * TERMS for _ in range(TERMS)]
    for n in range(TERMS):
        rest = list(cheb[n])
        for k in range(n, -1, -2):
            factor = rest[k] / basis[k][k]
            change[k][n] = factor
            for i, c in enumerate(basis[k]):
                rest[i] -= factor * c
    return change


CHANGE = basis_change()
CHEBYSHEV = [polynomial(n) for n in range(TERMS)]
POLYNOMIALS = [
    [math.fsum(CHANGE[k][n] * CHEBYSHEV[n][i] for n in range(k % 2, TERMS, 2)) for i in range(DEGREE + 1)]
    for k in range(TERMS)
]


def blocks_for(rows, most):
    return min(most, -(-rows // ROWS))


class Layout:
    def __init__(self, depth, tile_rows, width):
        self.depth = depth
        self.last = depth == STEPS - 1
        self.own = tile_rows // ROWS
        self.total = 2 * self.own
        self.width = width
        self.columns = width // LANES
        self.out_rows = tile_rows + MARGIN * (STEPS - 1 - depth)
        self.out_blocks = blocks_for(self.out_rows, self.total)

    def blocks(self, n):
        return blocks_for(self.out_rows + MARGIN - n, self.total)

    def state(self, n):
        return (4, self.blocks(n), ROWS, self.width)


def cols(j):
    return slice(j * LANES, (j + 1) * LANES)


def rows_at(block):
    return pl.ds(pl.multiple_of(block * ROWS, ROWS), ROWS)


class Order:
    def __init__(self, layout):
        self.layout = layout
        self.tile = lax.axis_index("tile")
        row = lax.broadcasted_iota(jnp.int32, (ROWS, LANES), 0)
        self.index = jnp.where(self.tile == 0, row, ROWS - 1 - row)

    def flip(self, x):
        return jnp.take_along_axis(x, self.index, axis=0)

    def own(self, b):
        return jnp.where(self.tile == 0, b, self.layout.own - 1 - b)

    def other(self, b):
        return jnp.where(self.tile == 0, b - self.layout.own, self.layout.total - 1 - b)


def recursion(layout, terms):
    lane = lax.broadcasted_iota(jnp.int32, (ROWS, LANES), 1)
    row = lax.broadcasted_iota(jnp.int32, (ROWS, LANES), 0)
    lane_first, lane_last = lane == 0, lane == LANES - 1
    row_first, row_last = row == 0, row == ROWS - 1
    zero = jnp.zeros((ROWS, LANES), jnp.float32)
    columns = range(layout.columns)

    def one_pass(n, c):
            source, count, have = terms[n - 1], layout.blocks(n), layout.blocks(n - 1)
            here = [source[c, 0, :, cols(j)] for j in columns]
            here_up = [pltpu.roll(x, ROWS - 1, 0) for x in here]
            before = here
            for b in range(count):
                if b + 1 < have:
                    below = [source[c, b + 1, :, cols(j)] for j in columns]
                    below_up = [pltpu.roll(x, ROWS - 1, 0) for x in below]
                else:
                    below = below_up = [zero] * layout.columns
                pairs = [p + jnp.where(row_last, q, r) for p, q, r in zip(here, below_up, here_up)]
                pairs_down = [pltpu.roll(u, 1, 0) for u in pairs]
                x = [u + jnp.where(row_first, q, r) for u, q, r in zip(pairs, before, pairs_down)]
                before = pairs_down
                x_left = [pltpu.roll(v, LANES - 1, 1) for v in x] + [zero]
                x_right = [pltpu.roll(v, 1, 1) for v in x] + [zero]
                wide = [
                    (x[j] + x[j])
                    + (
                        jnp.where(lane_last, x_left[j + 1], x_left[j])
                        + jnp.where(lane_first, x_right[j - 1], x_right[j])
                    )
                    for j in columns
                ]
                for j in columns:
                    value = wide[j] - 8.0 * here[j]
                    if n % 2 == 0 and ROOTS[n // 2 - 1] != 0.0:
                        value = value - (64.0 * ROOTS[n // 2 - 1]) * terms[n - 2][c, b, :, cols(j)]
                    terms[n][c, b, :, cols(j)] = value
                here, here_up = below, below_up

    for n in range(1, TERMS):
        for c in range(4):
            one_pass(n, c)


def combine(layout, scales, omega, slow_ref, terms, next_ref, maps_ref, beyond):
    order = Order(layout)
    start, stop = (layout.own, layout.out_blocks) if beyond else (0, layout.own)

    def one_block(b, carry):
        at = order.other(b) if beyond else order.own(b)
        for j in range(layout.columns):
            product = order.flip(slow_ref[j, layout.depth, rows_at(at), :]) * omega
            u = product * product * (2.0 / LARGEST**2) - 1.0
            sums = [None] * 4
            for n in range(TERMS):
                value = u * POLYNOMIALS[n][DEGREE] + POLYNOMIALS[n][DEGREE - 1]
                for k in range(DEGREE - 2, -1, -1):
                    value = value * u + POLYNOMIALS[n][k]
                if n % 2 == 1:
                    value = value * product
                for c in range(4):
                    if n % 2 == 0:
                        part = value * terms[n][c, b, :, cols(j)]
                        sums[c] = part if n == 0 else sums[c] + part
                    else:
                        part = value * terms[n][c ^ 1, b, :, cols(j)]
                        sums[c] = sums[c] - part if c in (0, 3) else sums[c] + part
            if next_ref is not None:
                for c in range(4):
                    next_ref[c, b, :, cols(j)] = sums[c]
            if not beyond:
                s_re, s_im, r_re, r_im = sums
                image = (s_re * r_re + s_im * r_im) * scales[0]
                energy = (s_re * s_re + s_im * s_im) * scales[1]
                maps_ref[rows_at(at), cols(j)] = order.flip(image)
                maps_ref[rows_at(layout.own + at), cols(j)] = order.flip(energy)
        return carry

    lax.fori_loop(start, stop, one_block, None)


VMEM = pl.BlockSpec(memory_space=pltpu.VMEM)
SMEM = pl.BlockSpec(memory_space=pltpu.SMEM)


def cost(flops):
    return pl.CostEstimate(flops=flops, bytes_accessed=2**20, transcendentals=0)


def first_terms(layout, source, receiver, other_source, other_receiver):
    def body(*refs):
        given, terms = refs[:4], refs[4:]
        order = Order(layout)
        for b in range(layout.blocks(0)):
            near = b < layout.own
            at = order.own(b) if near else order.other(b)
            for c in range(4):
                field = given[c // 2 + (0 if near else 2)]
                for j in range(layout.columns):
                    terms[0][c, b, :, cols(j)] = order.flip(field[c % 2, 0, rows_at(at), cols(j)])
        recursion(layout, terms)

    return pl.pallas_call(
        body,
        out_shape=[jax.ShapeDtypeStruct(layout.state(n), jnp.float32) for n in range(TERMS)],
        in_specs=[VMEM] * 4,
        out_specs=[VMEM] * TERMS,
        compiler_params=pltpu.CompilerParams(vmem_limit_bytes=16 * 2**20),
        cost_estimate=cost(8 * 10**9),
        name="first_terms",
    )(source, receiver, other_source, other_receiver)


def state(blocks, width):
    return jax.ShapeDtypeStruct((4, blocks, ROWS, width), jnp.float32)


def maps_shape(layout):
    return jax.ShapeDtypeStruct((2 * layout.own * ROWS, layout.width), jnp.float32)


def first_depth(layout, scales, omegas, terms, slow, other_slow):
    def body(omega_ref, slow_ref, other_ref, *refs):
        terms, maps_ref, next_ref = refs[:TERMS], refs[TERMS], refs[TERMS + 1]
        combine(layout, scales, omega_ref[0], slow_ref, terms, next_ref, maps_ref, False)
        combine(layout, scales, omega_ref[0], other_ref, terms, next_ref, None, True)

    return pl.pallas_call(
        body,
        out_shape=[maps_shape(layout), state(layout.out_blocks, layout.width)],
        in_specs=[SMEM] + [VMEM] * (2 + TERMS),
        out_specs=[VMEM] * 2,
        compiler_params=pltpu.CompilerParams(vmem_limit_bytes=16 * 2**20),
        cost_estimate=cost(3 * 10**9),
        name="first_depth",
    )(omegas, slow, other_slow, *terms)


def later_depth(layout, scales, omegas, fields, slow, other_slow):
    reaches = not layout.last

    def body(omega_ref, *refs):
        refs = list(refs)
        slow_ref = refs.pop(0)
        other_ref = refs.pop(0) if reaches else None
        fields_ref = refs.pop(0)
        maps_ref = refs.pop(0)
        next_ref = refs.pop(0) if reaches else None
        terms = [fields_ref] + refs
        recursion(layout, terms)
        combine(layout, scales, omega_ref[0], slow_ref, terms, next_ref, maps_ref, False)
        if reaches:
            combine(layout, scales, omega_ref[0], other_ref, terms, next_ref, None, True)

    out_shape = [maps_shape(layout)] + ([state(layout.out_blocks, layout.width)] if reaches else [])
    operands = [omegas, slow] + ([other_slow] if reaches else []) + [fields]
    return pl.pallas_call(
        body,
        out_shape=out_shape,
        in_specs=[SMEM] + [VMEM] * (len(operands) - 1),
        out_specs=[VMEM] * len(out_shape),
        scratch_shapes=[pltpu.VMEM(layout.state(n), jnp.float32) for n in range(1, TERMS)],
        compiler_params=pltpu.CompilerParams(vmem_limit_bytes=16 * 2**20),
        cost_estimate=cost(6 * 10**9),
        name="later_depth",
    )(*operands)


def gather(shard, axis):
    count = lax.axis_size(axis)
    return lax.all_to_all(jnp.broadcast_to(shard[None], (count,) + shard.shape), axis, 0, 0)


ANY = pl.BlockSpec(memory_space=pl.ANY)


def assemble(summed, tile_rows, width):
    count, steps, chunk = summed.shape[:3]
    direct = chunk % ROWS == 0

    def body(summed_ref, image_ref, energy_ref, staged, sems):
        copies = []

        def copy(piece, depth, at):
            out_ref, at = (image_ref, at) if at < tile_rows else (energy_ref, at - tile_rows)
            target = out_ref.at[depth, pl.ds(at, piece.shape[0])]
            copies.append(pltpu.make_async_copy(piece, target, sems.at[len(copies)]))
            copies[-1].start()

        for depth in range(steps):
            if direct:
                for source in range(count):
                    copy(summed_ref.at[source, depth], depth, source * chunk)
            else:
                for source in range(count):
                    staged[depth, source * chunk : (source + 1) * chunk] = summed_ref[source, depth]
                for at in (0, tile_rows):
                    copy(staged.at[depth, pl.ds(at, tile_rows)], depth, at)
        for each in copies:
            each.wait()

    shape = jax.ShapeDtypeStruct((steps, tile_rows, width), jnp.float32)
    return pl.pallas_call(
        body,
        out_shape=[shape, shape],
        in_specs=[ANY if direct else VMEM],
        out_specs=[ANY] * 2,
        scratch_shapes=[
            pltpu.VMEM((steps, 2 * tile_rows, width), jnp.float32),
            pltpu.SemaphoreType.DMA((steps * count,)),
        ],
        compiler_params=pltpu.CompilerParams(vmem_limit_bytes=8 * 2**20),
        cost_estimate=cost(10**8),
        name="assemble",
    )(summed)


def per_device(source_field, receiver_field, slowness, omegas):
    tiles = lax.axis_size("tile")
    assert tiles == 2
    swap = [(0, 1), (1, 0)]
    freqs = lax.axis_size("freq")
    tile_rows, width = source_field.shape[2], source_field.shape[3]
    scales = (1.0 / math.sqrt(omegas.shape[0] * freqs), 1.0 / (omegas.shape[0] * freqs))
    layouts = [Layout(depth, tile_rows, width) for depth in range(STEPS)]

    other_source = lax.ppermute(source_field, "tile", swap)
    other_receiver = lax.ppermute(receiver_field, "tile", swap)
    slow = gather(slowness, "freq")
    terms = first_terms(layouts[0], source_field, receiver_field, other_source, other_receiver)
    if slow.shape[-1] != LANES:
        slow = jnp.moveaxis(slow, 0, 2).reshape(STEPS, tile_rows, width // LANES, LANES)
        slow = jnp.moveaxis(slow, 2, 0)
    other_slow = lax.ppermute(slow, "tile", swap)

    chunk = 2 * tile_rows // freqs
    maps, fields = first_depth(layouts[0], scales, omegas, terms, slow, other_slow)
    every = [maps]
    for depth in range(1, STEPS):
        maps, *rest = later_depth(layouts[depth], scales, omegas, fields, slow, other_slow)
        fields = rest[0] if rest else None
        every.append(maps)
    parts = jnp.stack([maps.reshape(freqs, chunk, width) for maps in every], 1)
    reduced = jnp.sum(lax.all_to_all(parts, "freq", 0, 0), axis=0)
    return tuple(assemble(gather(reduced, "freq"), tile_rows, width))


def solution(mesh):
    in_specs = (
        P("shot", "freq", "tile", None),
        P("shot", "freq", "tile", None),
        P(None, "tile", "freq"),
        P("freq"),
    )
    out_specs = (P("shot", "tile", None), P("shot", "tile", None))
    return jax.shard_map(
        per_device, mesh=mesh, in_specs=in_specs, out_specs=out_specs, check_vma=False
    )
```

```python
import math

import jax
import jax.numpy as jnp
from jax import lax
from jax.experimental import pallas as pl
from jax.experimental.pallas import tpu as pltpu
from jax.sharding import PartitionSpec as P

STEPS = 3
TERMS = 10
NODES = 16
MARGIN = TERMS - 1
LANES = 128
ROWS = 8

LARGEST = 10.02
DEGREE = 11


def node_sum(order, product):
    wave = math.cos if order % 2 == 0 else math.sin
    weight = (1.0 if order == 0 else 2.0) / NODES
    angles = [math.pi * (m + 0.5) / NODES for m in range(NODES)]
    return weight * math.fsum(wave(product * math.cos(t)) * math.cos(order * t) for t in angles)


def polynomial(order):
    count = 64
    angles = [math.pi * (k + 0.5) / count for k in range(count)]
    samples = []
    for angle in angles:
        product = LARGEST * math.sqrt(0.5 * (math.cos(angle) + 1.0))
        value = node_sum(order, product)
        samples.append(value if order % 2 == 0 else value / product)
    cheb = [
        (1.0 if n == 0 else 2.0) / count * math.fsum(s * math.cos(n * t) for s, t in zip(samples, angles))
        for n in range(DEGREE + 1)
    ]
    powers = [0.0] * (DEGREE + 1)
    before, here = [1.0], [0.0, 1.0]
    for n in range(DEGREE + 1):
        now = before if n == 0 else here
        for k, c in enumerate(now):
            powers[k] += cheb[n] * c
        if n >= 1:
            after = [0.0] + [2.0 * c for c in here]
            for k, c in enumerate(before):
                after[k] -= c
            before, here = here, after
    return powers


ROOTS = (0.0, 0.95, 0.4, 0.75)


def basis_change():
    half = TERMS // 2

    def times(poly, factor):
        out = [0.0] * (len(poly) + len(factor) - 1)
        for i, a in enumerate(poly):
            for j, b in enumerate(factor):
                out[i + j] += a * b
        return out

    basis = [[1.0]]
    for n in range(1, TERMS):
        if n % 2 == 1:
            basis.append(times(basis[-1], [0.0, 8.0]))
        else:
            basis.append(times(basis[n - 2], [-64.0 * ROOTS[n // 2 - 1], 0.0, 64.0]))
    cheb = [[1.0], [0.0, 1.0]]
    for n in range(2, TERMS):
        new = [0.0] + [2.0 * c for c in cheb[-1]]
        for k, c in enumerate(cheb[n - 2]):
            new[k] -= c
        cheb.append(new)
    change = [[0.0] * TERMS for _ in range(TERMS)]
    for n in range(TERMS):
        rest = list(cheb[n])
        for k in range(n, -1, -2):
            factor = rest[k] / basis[k][k]
            change[k][n] = factor
            for i, c in enumerate(basis[k]):
                rest[i] -= factor * c
    return change


CHANGE = basis_change()
CHEBYSHEV = [polynomial(n) for n in range(TERMS)]
POLYNOMIALS = [
    [math.fsum(CHANGE[k][n] * CHEBYSHEV[n][i] for n in range(k % 2, TERMS, 2)) for i in range(DEGREE + 1)]
    for k in range(TERMS)
]


def blocks_for(rows, most):
    return min(most, -(-rows // ROWS))


class Layout:
    def __init__(self, depth, tile_rows, width):
        self.depth = depth
        self.last = depth == STEPS - 1
        self.own = tile_rows // ROWS
        self.total = 2 * self.own
        self.width = width
        self.columns = width // LANES
        self.out_rows = tile_rows + MARGIN * (STEPS - 1 - depth)
        self.out_blocks = blocks_for(self.out_rows, self.total)

    def blocks(self, n):
        return blocks_for(self.out_rows + MARGIN - n, self.total)

    def state(self, n):
        return (4, self.blocks(n), ROWS, self.width)


def cols(j):
    return slice(j * LANES, (j + 1) * LANES)


def rows_at(block):
    return pl.ds(pl.multiple_of(block * ROWS, ROWS), ROWS)


class Order:
    def __init__(self, layout):
        self.layout = layout
        self.tile = lax.axis_index("tile")
        row = lax.broadcasted_iota(jnp.int32, (ROWS, LANES), 0)
        self.index = jnp.where(self.tile == 0, row, ROWS - 1 - row)

    def flip(self, x):
        return jnp.take_along_axis(x, self.index, axis=0)

    def own(self, b):
        return jnp.where(self.tile == 0, b, self.layout.own - 1 - b)

    def other(self, b):
        return jnp.where(self.tile == 0, b - self.layout.own, self.layout.total - 1 - b)


def recursion(layout, terms):
    lane = lax.broadcasted_iota(jnp.int32, (ROWS, LANES), 1)
    row = lax.broadcasted_iota(jnp.int32, (ROWS, LANES), 0)
    lane_first, lane_last = lane == 0, lane == LANES - 1
    row_first, row_last = row == 0, row == ROWS - 1
    zero = jnp.zeros((ROWS, LANES), jnp.float32)
    columns = range(layout.columns)

    def one_pass(n, c):
            source, count, have = terms[n - 1], layout.blocks(n), layout.blocks(n - 1)
            here = [source[c, 0, :, cols(j)] for j in columns]
            here_up = [pltpu.roll(x, ROWS - 1, 0) for x in here]
            before = here
            for b in range(count):
                if b + 1 < have:
                    below = [source[c, b + 1, :, cols(j)] for j in columns]
                    below_up = [pltpu.roll(x, ROWS - 1, 0) for x in below]
                else:
                    below = below_up = [zero] * layout.columns
                pairs = [p + jnp.where(row_last, q, r) for p, q, r in zip(here, below_up, here_up)]
                pairs_down = [pltpu.roll(u, 1, 0) for u in pairs]
                x = [u + jnp.where(row_first, q, r) for u, q, r in zip(pairs, before, pairs_down)]
                before = pairs_down
                x_left = [pltpu.roll(v, LANES - 1, 1) for v in x] + [zero]
                x_right = [pltpu.roll(v, 1, 1) for v in x] + [zero]
                wide = [
                    (x[j] + x[j])
                    + (
                        jnp.where(lane_last, x_left[j + 1], x_left[j])
                        + jnp.where(lane_first, x_right[j - 1], x_right[j])
                    )
                    for j in columns
                ]
                for j in columns:
                    value = wide[j] - 8.0 * here[j]
                    if n % 2 == 0 and ROOTS[n // 2 - 1] != 0.0:
                        value = value - (64.0 * ROOTS[n // 2 - 1]) * terms[n - 2][c, b, :, cols(j)]
                    terms[n][c, b, :, cols(j)] = value
                here, here_up = below, below_up

    for n in range(1, TERMS):
        for c in range(4):
            one_pass(n, c)


def combine(layout, scales, omega, slow_ref, terms, next_ref, maps_ref, beyond):
    order = Order(layout)
    start, stop = (layout.own, layout.out_blocks) if beyond else (0, layout.own)

    def one_block(b, carry):
        at = order.other(b) if beyond else order.own(b)
        for j in range(layout.columns):
            product = order.flip(slow_ref[j, layout.depth, rows_at(at), :]) * omega
            u = product * product * (2.0 / LARGEST**2) - 1.0
            sums = [None] * 4
            for n in range(TERMS):
                value = u * POLYNOMIALS[n][DEGREE] + POLYNOMIALS[n][DEGREE - 1]
                for k in range(DEGREE - 2, -1, -1):
                    value = value * u + POLYNOMIALS[n][k]
                if n % 2 == 1:
                    value = value * product
                for c in range(4):
                    if n % 2 == 0:
                        part = value * terms[n][c, b, :, cols(j)]
                        sums[c] = part if n == 0 else sums[c] + part
                    else:
                        part = value * terms[n][c ^ 1, b, :, cols(j)]
                        sums[c] = sums[c] - part if c in (0, 3) else sums[c] + part
            if next_ref is not None:
                for c in range(4):
                    next_ref[c, b, :, cols(j)] = sums[c]
            if not beyond:
                s_re, s_im, r_re, r_im = sums
                image = (s_re * r_re + s_im * r_im) * scales[0]
                energy = (s_re * s_re + s_im * s_im) * scales[1]
                maps_ref[rows_at(at), cols(j)] = order.flip(image)
                maps_ref[rows_at(layout.own + at), cols(j)] = order.flip(energy)
        return carry

    lax.fori_loop(start, stop, one_block, None)


VMEM = pl.BlockSpec(memory_space=pltpu.VMEM)
SMEM = pl.BlockSpec(memory_space=pltpu.SMEM)


def cost(flops):
    return pl.CostEstimate(flops=flops, bytes_accessed=2**20, transcendentals=0)


def first_terms(layout, source, receiver, other_source, other_receiver):
    def body(*refs):
        given, terms = refs[:4], refs[4:]
        order = Order(layout)
        for b in range(layout.blocks(0)):
            near = b < layout.own
            at = order.own(b) if near else order.other(b)
            for c in range(4):
                field = given[c // 2 + (0 if near else 2)]
                for j in range(layout.columns):
                    terms[0][c, b, :, cols(j)] = order.flip(field[c % 2, 0, rows_at(at), cols(j)])
        recursion(layout, terms)

    return pl.pallas_call(
        body,
        out_shape=[jax.ShapeDtypeStruct(layout.state(n), jnp.float32) for n in range(TERMS)],
        in_specs=[VMEM] * 4,
        out_specs=[VMEM] * TERMS,
        compiler_params=pltpu.CompilerParams(vmem_limit_bytes=16 * 2**20),
        cost_estimate=cost(8 * 10**9),
        name="first_terms",
    )(source, receiver, other_source, other_receiver)


def state(blocks, width):
    return jax.ShapeDtypeStruct((4, blocks, ROWS, width), jnp.float32)


def maps_shape(layout):
    return jax.ShapeDtypeStruct((2 * layout.own * ROWS, layout.width), jnp.float32)


def first_depth(layout, scales, omegas, terms, slow, other_slow):
    def body(omega_ref, slow_ref, other_ref, *refs):
        terms, maps_ref, next_ref = refs[:TERMS], refs[TERMS], refs[TERMS + 1]
        combine(layout, scales, omega_ref[0], slow_ref, terms, next_ref, maps_ref, False)
        combine(layout, scales, omega_ref[0], other_ref, terms, next_ref, None, True)

    return pl.pallas_call(
        body,
        out_shape=[maps_shape(layout), state(layout.out_blocks, layout.width)],
        in_specs=[SMEM] + [VMEM] * (2 + TERMS),
        out_specs=[VMEM] * 2,
        compiler_params=pltpu.CompilerParams(vmem_limit_bytes=16 * 2**20),
        cost_estimate=cost(3 * 10**9),
        name="first_depth",
    )(omegas, slow, other_slow, *terms)


def later_depth(layout, scales, omegas, fields, slow, other_slow):
    reaches = not layout.last

    def body(omega_ref, *refs):
        refs = list(refs)
        slow_ref = refs.pop(0)
        other_ref = refs.pop(0) if reaches else None
        fields_ref = refs.pop(0)
        maps_ref = refs.pop(0)
        next_ref = refs.pop(0) if reaches else None
        terms = [fields_ref] + refs
        recursion(layout, terms)
        combine(layout, scales, omega_ref[0], slow_ref, terms, next_ref, maps_ref, False)
        if reaches:
            combine(layout, scales, omega_ref[0], other_ref, terms, next_ref, None, True)

    out_shape = [maps_shape(layout)] + ([state(layout.out_blocks, layout.width)] if reaches else [])
    operands = [omegas, slow] + ([other_slow] if reaches else []) + [fields]
    return pl.pallas_call(
        body,
        out_shape=out_shape,
        in_specs=[SMEM] + [VMEM] * (len(operands) - 1),
        out_specs=[VMEM] * len(out_shape),
        scratch_shapes=[pltpu.VMEM(layout.state(n), jnp.float32) for n in range(1, TERMS)],
        compiler_params=pltpu.CompilerParams(vmem_limit_bytes=16 * 2**20),
        cost_estimate=cost(6 * 10**9),
        name="later_depth",
    )(*operands)


def gather(shard, axis):
    count = lax.axis_size(axis)
    return lax.all_to_all(jnp.broadcast_to(shard[None], (count,) + shard.shape), axis, 0, 0)


ANY = pl.BlockSpec(memory_space=pl.ANY)


def halves(count):
    half = count // 2
    groups = [list(range(half)), list(range(half, count))]
    return half, groups, [(i, (i + half) % count) for i in range(count)]


def reduce_rows(maps, axis):
    half, groups, between = halves(lax.axis_size(axis))
    parts = lax.all_to_all(maps, axis, 0, 0, axis_index_groups=groups)
    summed = jnp.sum(parts, axis=0)
    upper = lax.axis_index(axis) >= half
    mine = jnp.where(upper, summed[1], summed[0])
    theirs = jnp.where(upper, summed[0], summed[1])
    return mine + lax.ppermute(theirs, axis, between)


def gather_rows(rows, axis):
    half, groups, between = halves(lax.axis_size(axis))
    pair = jnp.stack([rows, lax.ppermute(rows, axis, between)])
    return lax.all_to_all(
        jnp.broadcast_to(pair[None], (half,) + pair.shape), axis, 0, 0, axis_index_groups=groups
    )


def assemble(gathered, tile_rows, width):
    half, _, steps, chunk = gathered.shape[:4]
    direct = chunk % ROWS == 0

    def body(gathered_ref, image_ref, energy_ref, staged, sems):
        upper = (lax.axis_index("freq") >= half).astype(jnp.int32)
        copies = []

        def copy(piece, depth, start, offset):
            out_ref, start = (image_ref, start) if start < tile_rows else (energy_ref, start - tile_rows)
            target = out_ref.at[depth, pl.ds(start + offset, piece.shape[0])]
            copies.append(pltpu.make_async_copy(piece, target, sems.at[len(copies)]))
            copies[-1].start()

        for depth in range(steps):
            if direct:
                for p in range(half):
                    for k in range(2):
                        offset = pl.multiple_of((upper ^ k) * chunk, chunk)
                        copy(gathered_ref.at[p, k, depth], depth, 2 * p * chunk, offset)
            else:
                for p in range(half):
                    for k in range(2):
                        start = (2 * p + k) * chunk
                        staged[depth, start : start + chunk] = jnp.where(
                            upper == 0, gathered_ref[p, k, depth], gathered_ref[p, 1 - k, depth]
                        )
                for start in (0, tile_rows):
                    copy(staged.at[depth, pl.ds(start, tile_rows)], depth, start, 0)
        for each in copies:
            each.wait()

    shape = jax.ShapeDtypeStruct((steps, tile_rows, width), jnp.float32)
    return pl.pallas_call(
        body,
        out_shape=[shape, shape],
        in_specs=[ANY if direct else VMEM],
        out_specs=[ANY] * 2,
        scratch_shapes=[
            pltpu.VMEM((steps, 2 * tile_rows, width), jnp.float32),
            pltpu.SemaphoreType.DMA((steps * 2 * half,)),
        ],
        compiler_params=pltpu.CompilerParams(vmem_limit_bytes=8 * 2**20),
        cost_estimate=cost(10**8),
        name="assemble",
    )(gathered)


def per_device(source_field, receiver_field, slowness, omegas):
    tiles = lax.axis_size("tile")
    assert tiles == 2
    swap = [(0, 1), (1, 0)]
    freqs = lax.axis_size("freq")
    tile_rows, width = source_field.shape[2], source_field.shape[3]
    scales = (1.0 / math.sqrt(omegas.shape[0] * freqs), 1.0 / (omegas.shape[0] * freqs))
    layouts = [Layout(depth, tile_rows, width) for depth in range(STEPS)]

    other_source = lax.ppermute(source_field, "tile", swap)
    other_receiver = lax.ppermute(receiver_field, "tile", swap)
    slow = gather(slowness, "freq")
    terms = first_terms(layouts[0], source_field, receiver_field, other_source, other_receiver)
    if slow.shape[-1] != LANES:
        slow = jnp.moveaxis(slow, 0, 2).reshape(STEPS, tile_rows, width // LANES, LANES)
        slow = jnp.moveaxis(slow, 2, 0)
    other_slow = lax.ppermute(slow, "tile", swap)

    chunk = 2 * tile_rows // freqs
    maps, fields = first_depth(layouts[0], scales, omegas, terms, slow, other_slow)
    every = [maps]
    for depth in range(1, STEPS):
        maps, *rest = later_depth(layouts[depth], scales, omegas, fields, slow, other_slow)
        fields = rest[0] if rest else None
        every.append(maps)
    parts = jnp.stack([maps.reshape(freqs // 2, 2, chunk, width) for maps in every], 2)
    return tuple(assemble(gather_rows(reduce_rows(parts, "freq"), "freq"), tile_rows, width))


def solution(mesh):
    in_specs = (
        P("shot", "freq", "tile", None),
        P("shot", "freq", "tile", None),
        P(None, "tile", "freq"),
        P("freq"),
    )
    out_specs = (P("shot", "tile", None), P("shot", "tile", None))
    return jax.shard_map(
        per_device, mesh=mesh, in_specs=in_specs, out_specs=out_specs, check_vma=False
    )
```

```python
import math

import jax
import jax.numpy as jnp
from jax import lax
from jax.experimental import pallas as pl
from jax.experimental.pallas import tpu as pltpu
from jax.sharding import PartitionSpec as P

STEPS = 3
TERMS = 10
NODES = 16
MARGIN = TERMS - 1
LANES = 128
ROWS = 8

LARGEST = 10.02
DEGREE = 11


def node_sum(order, product):
    wave = math.cos if order % 2 == 0 else math.sin
    weight = (1.0 if order == 0 else 2.0) / NODES
    angles = [math.pi * (m + 0.5) / NODES for m in range(NODES)]
    return weight * math.fsum(wave(product * math.cos(t)) * math.cos(order * t) for t in angles)


def polynomial(order):
    count = 64
    angles = [math.pi * (k + 0.5) / count for k in range(count)]
    samples = []
    for angle in angles:
        product = LARGEST * math.sqrt(0.5 * (math.cos(angle) + 1.0))
        value = node_sum(order, product)
        samples.append(value if order % 2 == 0 else value / product)
    cheb = [
        (1.0 if n == 0 else 2.0) / count * math.fsum(s * math.cos(n * t) for s, t in zip(samples, angles))
        for n in range(DEGREE + 1)
    ]
    powers = [0.0] * (DEGREE + 1)
    before, here = [1.0], [0.0, 1.0]
    for n in range(DEGREE + 1):
        now = before if n == 0 else here
        for k, c in enumerate(now):
            powers[k] += cheb[n] * c
        if n >= 1:
            after = [0.0] + [2.0 * c for c in here]
            for k, c in enumerate(before):
                after[k] -= c
            before, here = here, after
    return powers


ROOTS = (0.0, 0.95, 0.4, 0.75)


def basis_change():
    half = TERMS // 2

    def times(poly, factor):
        out = [0.0] * (len(poly) + len(factor) - 1)
        for i, a in enumerate(poly):
            for j, b in enumerate(factor):
                out[i + j] += a * b
        return out

    basis = [[1.0]]
    for n in range(1, TERMS):
        if n % 2 == 1:
            basis.append(times(basis[-1], [0.0, 8.0]))
        else:
            basis.append(times(basis[n - 2], [-64.0 * ROOTS[n // 2 - 1], 0.0, 64.0]))
    cheb = [[1.0], [0.0, 1.0]]
    for n in range(2, TERMS):
        new = [0.0] + [2.0 * c for c in cheb[-1]]
        for k, c in enumerate(cheb[n - 2]):
            new[k] -= c
        cheb.append(new)
    change = [[0.0] * TERMS for _ in range(TERMS)]
    for n in range(TERMS):
        rest = list(cheb[n])
        for k in range(n, -1, -2):
            factor = rest[k] / basis[k][k]
            change[k][n] = factor
            for i, c in enumerate(basis[k]):
                rest[i] -= factor * c
    return change


CHANGE = basis_change()
CHEBYSHEV = [polynomial(n) for n in range(TERMS)]
POLYNOMIALS = [
    [math.fsum(CHANGE[k][n] * CHEBYSHEV[n][i] for n in range(k % 2, TERMS, 2)) for i in range(DEGREE + 1)]
    for k in range(TERMS)
]


def blocks_for(rows, most):
    return min(most, -(-rows // ROWS))


class Layout:
    def __init__(self, depth, tile_rows, width):
        self.depth = depth
        self.last = depth == STEPS - 1
        self.own = tile_rows // ROWS
        self.total = 2 * self.own
        self.width = width
        self.columns = width // LANES
        self.out_rows = tile_rows + MARGIN * (STEPS - 1 - depth)
        self.out_blocks = blocks_for(self.out_rows, self.total)

    def blocks(self, n):
        return blocks_for(self.out_rows + MARGIN - n, self.total)

    def state(self, n):
        return (4, self.blocks(n), ROWS, self.width)


def cols(j):
    return slice(j * LANES, (j + 1) * LANES)


def rows_at(block):
    return pl.ds(pl.multiple_of(block * ROWS, ROWS), ROWS)


class Order:
    def __init__(self, layout):
        self.layout = layout
        self.tile = lax.axis_index("tile")
        row = lax.broadcasted_iota(jnp.int32, (ROWS, LANES), 0)
        self.index = jnp.where(self.tile == 0, row, ROWS - 1 - row)

    def flip(self, x):
        return jnp.take_along_axis(x, self.index, axis=0)

    def own(self, b):
        return jnp.where(self.tile == 0, b, self.layout.own - 1 - b)

    def other(self, b):
        return jnp.where(self.tile == 0, b - self.layout.own, self.layout.total - 1 - b)


def recursion(layout, terms):
    lane = lax.broadcasted_iota(jnp.int32, (ROWS, LANES), 1)
    row = lax.broadcasted_iota(jnp.int32, (ROWS, LANES), 0)
    lane_first, lane_last = lane == 0, lane == LANES - 1
    row_first, row_last = row == 0, row == ROWS - 1
    zero = jnp.zeros((ROWS, LANES), jnp.float32)
    columns = range(layout.columns)

    def one_pass(n, c):
            source, count, have = terms[n - 1], layout.blocks(n), layout.blocks(n - 1)
            here = [source[c, 0, :, cols(j)] for j in columns]
            here_up = [pltpu.roll(x, ROWS - 1, 0) for x in here]
            before = here
            for b in range(count):
                if b + 1 < have:
                    below = [source[c, b + 1, :, cols(j)] for j in columns]
                    below_up = [pltpu.roll(x, ROWS - 1, 0) for x in below]
                else:
                    below = below_up = [zero] * layout.columns
                pairs = [p + jnp.where(row_last, q, r) for p, q, r in zip(here, below_up, here_up)]
                pairs_down = [pltpu.roll(u, 1, 0) for u in pairs]
                x = [u + jnp.where(row_first, q, r) for u, q, r in zip(pairs, before, pairs_down)]
                before = pairs_down
                x_left = [pltpu.roll(v, LANES - 1, 1) for v in x] + [zero]
                x_right = [pltpu.roll(v, 1, 1) for v in x] + [zero]
                wide = [
                    (x[j] + x[j])
                    + (
                        jnp.where(lane_last, x_left[j + 1], x_left[j])
                        + jnp.where(lane_first, x_right[j - 1], x_right[j])
                    )
                    for j in columns
                ]
                for j in columns:
                    value = wide[j] - 8.0 * here[j]
                    if n % 2 == 0 and ROOTS[n // 2 - 1] != 0.0:
                        value = value - (64.0 * ROOTS[n // 2 - 1]) * terms[n - 2][c, b, :, cols(j)]
                    terms[n][c, b, :, cols(j)] = value
                here, here_up = below, below_up

    for n in range(1, TERMS):
        for c in range(4):
            one_pass(n, c)


def combine(layout, scales, omega, slow_ref, terms, next_ref, maps_ref, beyond):
    order = Order(layout)
    upper = in_upper_half("freq").astype(jnp.int32)
    start, stop = (layout.own, layout.out_blocks) if beyond else (0, layout.own)

    def one_block(b, carry):
        at = order.other(b) if beyond else order.own(b)
        for j in range(layout.columns):
            p, k = j % (layout.columns // 2), j // (layout.columns // 2)
            product = order.flip(slow_ref[p, k ^ upper, layout.depth, rows_at(at), :]) * omega
            u = product * product * (2.0 / LARGEST**2) - 1.0
            sums = [None] * 4
            for n in range(TERMS):
                value = u * POLYNOMIALS[n][DEGREE] + POLYNOMIALS[n][DEGREE - 1]
                for k in range(DEGREE - 2, -1, -1):
                    value = value * u + POLYNOMIALS[n][k]
                if n % 2 == 1:
                    value = value * product
                for c in range(4):
                    if n % 2 == 0:
                        part = value * terms[n][c, b, :, cols(j)]
                        sums[c] = part if n == 0 else sums[c] + part
                    else:
                        part = value * terms[n][c ^ 1, b, :, cols(j)]
                        sums[c] = sums[c] - part if c in (0, 3) else sums[c] + part
            if next_ref is not None:
                for c in range(4):
                    next_ref[c, b, :, cols(j)] = sums[c]
            if not beyond:
                s_re, s_im, r_re, r_im = sums
                image = (s_re * r_re + s_im * r_im) * scales[0]
                energy = (s_re * s_re + s_im * s_im) * scales[1]
                maps_ref[rows_at(at), cols(j)] = order.flip(image)
                maps_ref[rows_at(layout.own + at), cols(j)] = order.flip(energy)
        return carry

    lax.fori_loop(start, stop, one_block, None)


VMEM = pl.BlockSpec(memory_space=pltpu.VMEM)
SMEM = pl.BlockSpec(memory_space=pltpu.SMEM)
ANY = pl.BlockSpec(memory_space=pl.ANY)


def cost(flops):
    return pl.CostEstimate(flops=flops, bytes_accessed=2**20, transcendentals=0)


def first_terms(layout, source, receiver, other_source, other_receiver):
    def body(*refs):
        given, terms = refs[:4], refs[4:]
        order = Order(layout)
        for b in range(layout.blocks(0)):
            near = b < layout.own
            at = order.own(b) if near else order.other(b)
            for c in range(4):
                field = given[c // 2 + (0 if near else 2)]
                for j in range(layout.columns):
                    terms[0][c, b, :, cols(j)] = order.flip(field[c % 2, 0, rows_at(at), cols(j)])
        recursion(layout, terms)

    return pl.pallas_call(
        body,
        out_shape=[jax.ShapeDtypeStruct(layout.state(n), jnp.float32) for n in range(TERMS)],
        in_specs=[VMEM] * 4,
        out_specs=[VMEM] * TERMS,
        compiler_params=pltpu.CompilerParams(vmem_limit_bytes=16 * 2**20),
        cost_estimate=cost(8 * 10**9),
        name="first_terms",
    )(source, receiver, other_source, other_receiver)


def state(blocks, width):
    return jax.ShapeDtypeStruct((4, blocks, ROWS, width), jnp.float32)


def maps_shape(layout):
    return jax.ShapeDtypeStruct((2 * layout.own * ROWS, layout.width), jnp.float32)


def first_depth(layout, scales, omegas, terms, slow, other_slow):
    def body(omega_ref, slow_ref, other_ref, *refs):
        terms, maps_ref, next_ref = refs[:TERMS], refs[TERMS], refs[TERMS + 1]
        combine(layout, scales, omega_ref[0], slow_ref, terms, next_ref, maps_ref, False)
        combine(layout, scales, omega_ref[0], other_ref, terms, next_ref, None, True)

    return pl.pallas_call(
        body,
        out_shape=[maps_shape(layout), state(layout.out_blocks, layout.width)],
        in_specs=[SMEM] + [VMEM] * (2 + TERMS),
        out_specs=[VMEM] * 2,
        compiler_params=pltpu.CompilerParams(vmem_limit_bytes=16 * 2**20),
        cost_estimate=cost(3 * 10**9),
        name="first_depth",
    )(omegas, slow, other_slow, *terms)


def later_depth(layout, scales, omegas, fields, slow, other_slow):
    reaches = not layout.last

    def body(omega_ref, *refs):
        refs = list(refs)
        slow_ref = refs.pop(0)
        other_ref = refs.pop(0) if reaches else None
        fields_ref = refs.pop(0)
        maps_ref = refs.pop(0)
        next_ref = refs.pop(0) if reaches else None
        terms = [fields_ref] + refs
        recursion(layout, terms)
        combine(layout, scales, omega_ref[0], slow_ref, terms, next_ref, maps_ref, False)
        if reaches:
            combine(layout, scales, omega_ref[0], other_ref, terms, next_ref, None, True)

    out_shape = [maps_shape(layout)] + ([state(layout.out_blocks, layout.width)] if reaches else [])
    operands = [omegas, slow] + ([other_slow] if reaches else []) + [fields]
    return pl.pallas_call(
        body,
        out_shape=out_shape,
        in_specs=[SMEM] + [VMEM] * (len(operands) - 1),
        out_specs=[VMEM] * len(out_shape),
        scratch_shapes=[pltpu.VMEM(layout.state(n), jnp.float32) for n in range(1, TERMS)],
        compiler_params=pltpu.CompilerParams(vmem_limit_bytes=16 * 2**20),
        cost_estimate=cost(6 * 10**9),
        name="later_depth",
    )(*operands)


def in_upper_half(axis):
    return lax.axis_index(axis) >= lax.axis_size(axis) // 2


def all_slowness(slowness, width):
    slow = gather_rows(slowness, "freq")
    if slowness.shape[-1] == LANES:
        return slow
    upper = in_upper_half("freq")
    slow = jnp.where(upper, slow[:, ::-1], slow)
    slow = jnp.moveaxis(slow, (1, 0), (2, 3)).reshape(slowness.shape[:2] + (2, width // LANES // 2, LANES))
    slow = jnp.moveaxis(slow, (3, 2), (0, 1))
    return jnp.where(upper, slow[:, ::-1], slow)


def halves(count):
    half = count // 2
    groups = [list(range(half)), list(range(half, count))]
    return half, groups, [(i, (i + half) % count) for i in range(count)]


def sum_rows(maps, axis):
    half, groups, between = halves(lax.axis_size(axis))
    flat = maps.reshape(half, -1, maps.shape[-1])
    parts = lax.all_to_all(flat, axis, 0, 0, axis_index_groups=groups)
    summed = jnp.sum(parts, axis=0)
    summed = summed + lax.ppermute(summed, axis, between)
    spread = jnp.broadcast_to(summed[None], (half,) + summed.shape)
    return lax.all_to_all(spread, axis, 0, 0, axis_index_groups=groups).reshape(maps.shape)


def gather_rows(rows, axis):
    half, groups, between = halves(lax.axis_size(axis))
    others = lax.ppermute(rows, axis, between)
    own = lax.broadcasted_iota(jnp.int32, (half, 2) + (1,) * rows.ndim, 1) == 0
    pairs = jnp.where(own, rows, others)
    flat = pairs.reshape(half, -1, rows.shape[-1])
    return lax.all_to_all(flat, axis, 0, 0, axis_index_groups=groups).reshape(pairs.shape)


def assemble(gathered, tile_rows, width):
    half, _, steps, chunk = gathered.shape[:4]
    direct = chunk % ROWS == 0

    def body(gathered_ref, image_ref, energy_ref, staged, sems):
        copies = []

        def copy(piece, depth, start):
            out_ref, start = (image_ref, start) if start < tile_rows else (energy_ref, start - tile_rows)
            target = out_ref.at[depth, pl.ds(start, piece.shape[0])]
            copies.append(pltpu.make_async_copy(piece, target, sems.at[len(copies)]))
            copies[-1].start()

        for depth in range(steps):
            if direct:
                for p in range(half):
                    for k in range(2):
                        copy(gathered_ref.at[p, k, depth], depth, (2 * p + k) * chunk)
            else:
                for p in range(half):
                    for k in range(2):
                        start = (2 * p + k) * chunk
                        staged[depth, start : start + chunk] = gathered_ref[p, k, depth]
                for start in (0, tile_rows):
                    copy(staged.at[depth, pl.ds(start, tile_rows)], depth, start)
        for each in copies:
            each.wait()

    shape = jax.ShapeDtypeStruct((steps, tile_rows, width), jnp.float32)
    return pl.pallas_call(
        body,
        out_shape=[shape, shape],
        in_specs=[ANY if direct else VMEM],
        out_specs=[ANY] * 2,
        scratch_shapes=[
            pltpu.VMEM((steps, 2 * tile_rows, width), jnp.float32),
            pltpu.SemaphoreType.DMA((steps * 2 * half,)),
        ],
        compiler_params=pltpu.CompilerParams(vmem_limit_bytes=8 * 2**20),
        cost_estimate=cost(10**8),
        name="assemble",
    )(gathered)


def per_device(source_field, receiver_field, slowness, omegas):
    tiles = lax.axis_size("tile")
    assert tiles == 2
    swap = [(0, 1), (1, 0)]
    freqs = lax.axis_size("freq")
    tile_rows, width = source_field.shape[2], source_field.shape[3]
    scales = (1.0 / math.sqrt(omegas.shape[0] * freqs), 1.0 / (omegas.shape[0] * freqs))
    layouts = [Layout(depth, tile_rows, width) for depth in range(STEPS)]

    other_source = lax.ppermute(source_field, "tile", swap)
    other_receiver = lax.ppermute(receiver_field, "tile", swap)
    slow = all_slowness(slowness, width)
    terms = first_terms(layouts[0], source_field, receiver_field, other_source, other_receiver)
    other_slow = lax.ppermute(slow, "tile", swap)

    chunk = 2 * tile_rows // freqs
    maps, fields = first_depth(layouts[0], scales, omegas, terms, slow, other_slow)
    every = [maps]
    for depth in range(1, STEPS):
        maps, *rest = later_depth(layouts[depth], scales, omegas, fields, slow, other_slow)
        fields = rest[0] if rest else None
        every.append(maps)
    parts = jnp.stack([maps.reshape(freqs // 2, 2, chunk, width) for maps in every], 2)
    return tuple(assemble(sum_rows(parts, "freq"), tile_rows, width))


def solution(mesh):
    in_specs = (
        P("shot", "freq", "tile", None),
        P("shot", "freq", "tile", None),
        P(None, "tile", "freq"),
        P("freq"),
    )
    out_specs = (P("shot", "tile", None), P("shot", "tile", None))
    return jax.shard_map(
        per_device, mesh=mesh, in_specs=in_specs, out_specs=out_specs, check_vma=False
    )
```

```python
import math

import jax
import jax.numpy as jnp
from jax import lax
from jax.experimental import pallas as pl
from jax.experimental.pallas import tpu as pltpu
from jax.sharding import PartitionSpec as P

STEPS = 3
TERMS = 10
NODES = 16
MARGIN = TERMS - 1
LANES = 128
ROWS = 8

LARGEST = 10.02
DEGREE = 11


def node_sum(order, product):
    wave = math.cos if order % 2 == 0 else math.sin
    weight = (1.0 if order == 0 else 2.0) / NODES
    angles = [math.pi * (m + 0.5) / NODES for m in range(NODES)]
    return weight * math.fsum(wave(product * math.cos(t)) * math.cos(order * t) for t in angles)


def polynomial(order):
    count = 64
    angles = [math.pi * (k + 0.5) / count for k in range(count)]
    samples = []
    for angle in angles:
        product = LARGEST * math.sqrt(0.5 * (math.cos(angle) + 1.0))
        value = node_sum(order, product)
        samples.append(value if order % 2 == 0 else value / product)
    cheb = [
        (1.0 if n == 0 else 2.0) / count * math.fsum(s * math.cos(n * t) for s, t in zip(samples, angles))
        for n in range(DEGREE + 1)
    ]
    powers = [0.0] * (DEGREE + 1)
    before, here = [1.0], [0.0, 1.0]
    for n in range(DEGREE + 1):
        now = before if n == 0 else here
        for k, c in enumerate(now):
            powers[k] += cheb[n] * c
        if n >= 1:
            after = [0.0] + [2.0 * c for c in here]
            for k, c in enumerate(before):
                after[k] -= c
            before, here = here, after
    return powers


ROOTS = (0.0, 0.95, 0.4, 0.75)


def basis_change():
    half = TERMS // 2

    def times(poly, factor):
        out = [0.0] * (len(poly) + len(factor) - 1)
        for i, a in enumerate(poly):
            for j, b in enumerate(factor):
                out[i + j] += a * b
        return out

    basis = [[1.0]]
    for n in range(1, TERMS):
        if n % 2 == 1:
            basis.append(times(basis[-1], [0.0, 8.0]))
        else:
            basis.append(times(basis[n - 2], [-64.0 * ROOTS[n // 2 - 1], 0.0, 64.0]))
    cheb = [[1.0], [0.0, 1.0]]
    for n in range(2, TERMS):
        new = [0.0] + [2.0 * c for c in cheb[-1]]
        for k, c in enumerate(cheb[n - 2]):
            new[k] -= c
        cheb.append(new)
    change = [[0.0] * TERMS for _ in range(TERMS)]
    for n in range(TERMS):
        rest = list(cheb[n])
        for k in range(n, -1, -2):
            factor = rest[k] / basis[k][k]
            change[k][n] = factor
            for i, c in enumerate(basis[k]):
                rest[i] -= factor * c
    return change


CHANGE = basis_change()
CHEBYSHEV = [polynomial(n) for n in range(TERMS)]
POLYNOMIALS = [
    [math.fsum(CHANGE[k][n] * CHEBYSHEV[n][i] for n in range(k % 2, TERMS, 2)) for i in range(DEGREE + 1)]
    for k in range(TERMS)
]


def blocks_for(rows, most):
    return min(most, -(-rows // ROWS))


class Layout:
    def __init__(self, depth, tile_rows, width):
        self.depth = depth
        self.last = depth == STEPS - 1
        self.own = tile_rows // ROWS
        self.total = 2 * self.own
        self.width = width
        self.columns = width // LANES
        self.out_rows = tile_rows + MARGIN * (STEPS - 1 - depth)
        self.out_blocks = blocks_for(self.out_rows, self.total)

    def blocks(self, n):
        return blocks_for(self.out_rows + MARGIN - n, self.total)

    def state(self, n):
        return (4, self.blocks(n), ROWS, self.width)


def cols(j):
    return slice(j * LANES, (j + 1) * LANES)


def rows_at(block):
    return pl.ds(pl.multiple_of(block * ROWS, ROWS), ROWS)


class Order:
    def __init__(self, layout):
        self.layout = layout
        self.tile = lax.axis_index("tile")
        row = lax.broadcasted_iota(jnp.int32, (ROWS, LANES), 0)
        self.index = jnp.where(self.tile == 0, row, ROWS - 1 - row)

    def flip(self, x):
        return jnp.take_along_axis(x, self.index, axis=0)

    def own(self, b):
        return jnp.where(self.tile == 0, b, self.layout.own - 1 - b)

    def other(self, b):
        return jnp.where(self.tile == 0, b - self.layout.own, self.layout.total - 1 - b)


def recursion(layout, terms):
    lane = lax.broadcasted_iota(jnp.int32, (ROWS, LANES), 1)
    row = lax.broadcasted_iota(jnp.int32, (ROWS, LANES), 0)
    lane_first, lane_last = lane == 0, lane == LANES - 1
    row_first, row_last = row == 0, row == ROWS - 1
    zero = jnp.zeros((ROWS, LANES), jnp.float32)
    columns = range(layout.columns)

    def one_pass(n, c):
        source, count, have = terms[n - 1], layout.blocks(n), layout.blocks(n - 1)

        def tile(b, j):
            return source[c, b, :, cols(j)] if b < have else zero

        up = [pltpu.roll(tile(0, j), ROWS - 1, 0) for j in columns]
        before = [None] * layout.columns
        for b in range(count):
            x, left, right = {}, {-1: zero}, {layout.columns: zero}

            def finish(j, b=b, x=x, left=left, right=right):
                low = jnp.where(lane_first, left[j - 1], left[j])
                high = jnp.where(lane_last, right[j + 1], right[j])
                value = (x[j] + x[j]) + (low + high) - 8.0 * tile(b, j)
                if n % 2 == 0 and ROOTS[n // 2 - 1] != 0.0:
                    value = value - (64.0 * ROOTS[n // 2 - 1]) * terms[n - 2][c, b, :, cols(j)]
                terms[n][c, b, :, cols(j)] = value

            for j in columns:
                p = tile(b, j)
                below = pltpu.roll(tile(b + 1, j), ROWS - 1, 0)
                pair = p + jnp.where(row_last, below, up[j])
                down = pltpu.roll(pair, 1, 0)
                x[j] = pair + jnp.where(row_first, p if b == 0 else before[j], down)
                up[j], before[j] = below, down
                left[j], right[j] = pltpu.roll(x[j], 1, 1), pltpu.roll(x[j], LANES - 1, 1)
                if j > 0:
                    finish(j - 1)
            finish(layout.columns - 1)

    for n in range(1, TERMS):
        for c in range(4):
            one_pass(n, c)


def combine(layout, scales, omega, slow_ref, terms, next_ref, maps_ref, beyond):
    order = Order(layout)
    upper = in_upper_half("freq").astype(jnp.int32)
    start, stop = (layout.own, layout.out_blocks) if beyond else (0, layout.own)

    def one_block(b, carry):
        at = order.other(b) if beyond else order.own(b)
        for j in range(layout.columns):
            p, k = j % (layout.columns // 2), j // (layout.columns // 2)
            product = order.flip(slow_ref[p, k ^ upper, layout.depth, rows_at(at), :]) * omega
            u = product * product * (2.0 / LARGEST**2) - 1.0
            sums = [None] * 4
            for n in range(TERMS):
                value = u * POLYNOMIALS[n][DEGREE] + POLYNOMIALS[n][DEGREE - 1]
                for k in range(DEGREE - 2, -1, -1):
                    value = value * u + POLYNOMIALS[n][k]
                if n % 2 == 1:
                    value = value * product
                for c in range(4):
                    if n % 2 == 0:
                        part = value * terms[n][c, b, :, cols(j)]
                        sums[c] = part if n == 0 else sums[c] + part
                    else:
                        part = value * terms[n][c ^ 1, b, :, cols(j)]
                        sums[c] = sums[c] - part if c in (0, 3) else sums[c] + part
            if next_ref is not None:
                for c in range(4):
                    next_ref[c, b, :, cols(j)] = sums[c]
            if not beyond:
                s_re, s_im, r_re, r_im = sums
                image = (s_re * r_re + s_im * r_im) * scales[0]
                energy = (s_re * s_re + s_im * s_im) * scales[1]
                maps_ref[rows_at(at), cols(j)] = order.flip(image)
                maps_ref[rows_at(layout.own + at), cols(j)] = order.flip(energy)
        return carry

    lax.fori_loop(start, stop, one_block, None)


VMEM = pl.BlockSpec(memory_space=pltpu.VMEM)
SMEM = pl.BlockSpec(memory_space=pltpu.SMEM)
ANY = pl.BlockSpec(memory_space=pl.ANY)


def cost(flops):
    return pl.CostEstimate(flops=flops, bytes_accessed=2**20, transcendentals=0)


def first_terms(layout, source, receiver, other_source, other_receiver):
    def body(*refs):
        given, terms = refs[:4], refs[4:]
        order = Order(layout)
        for b in range(layout.blocks(0)):
            near = b < layout.own
            at = order.own(b) if near else order.other(b)
            for c in range(4):
                field = given[c // 2 + (0 if near else 2)]
                for j in range(layout.columns):
                    terms[0][c, b, :, cols(j)] = order.flip(field[c % 2, 0, rows_at(at), cols(j)])
        recursion(layout, terms)

    return pl.pallas_call(
        body,
        out_shape=[jax.ShapeDtypeStruct(layout.state(n), jnp.float32) for n in range(TERMS)],
        in_specs=[VMEM] * 4,
        out_specs=[VMEM] * TERMS,
        compiler_params=pltpu.CompilerParams(vmem_limit_bytes=16 * 2**20),
        cost_estimate=cost(8 * 10**9),
        name="first_terms",
    )(source, receiver, other_source, other_receiver)


def state(blocks, width):
    return jax.ShapeDtypeStruct((4, blocks, ROWS, width), jnp.float32)


def maps_shape(layout):
    return jax.ShapeDtypeStruct((2 * layout.own * ROWS, layout.width), jnp.float32)


def first_depth(layout, scales, omegas, terms, slow, other_slow):
    def body(omega_ref, slow_ref, other_ref, *refs):
        terms, maps_ref, next_ref = refs[:TERMS], refs[TERMS], refs[TERMS + 1]
        combine(layout, scales, omega_ref[0], slow_ref, terms, next_ref, maps_ref, False)
        combine(layout, scales, omega_ref[0], other_ref, terms, next_ref, None, True)

    return pl.pallas_call(
        body,
        out_shape=[maps_shape(layout), state(layout.out_blocks, layout.width)],
        in_specs=[SMEM] + [VMEM] * (2 + TERMS),
        out_specs=[VMEM] * 2,
        compiler_params=pltpu.CompilerParams(vmem_limit_bytes=16 * 2**20),
        cost_estimate=cost(3 * 10**9),
        name="first_depth",
    )(omegas, slow, other_slow, *terms)


def later_depth(layout, scales, omegas, fields, slow, other_slow):
    reaches = not layout.last

    def body(omega_ref, *refs):
        refs = list(refs)
        slow_ref = refs.pop(0)
        other_ref = refs.pop(0) if reaches else None
        fields_ref = refs.pop(0)
        maps_ref = refs.pop(0)
        next_ref = refs.pop(0) if reaches else None
        terms = [fields_ref] + refs
        recursion(layout, terms)
        combine(layout, scales, omega_ref[0], slow_ref, terms, next_ref, maps_ref, False)
        if reaches:
            combine(layout, scales, omega_ref[0], other_ref, terms, next_ref, None, True)

    out_shape = [maps_shape(layout)] + ([state(layout.out_blocks, layout.width)] if reaches else [])
    operands = [omegas, slow] + ([other_slow] if reaches else []) + [fields]
    return pl.pallas_call(
        body,
        out_shape=out_shape,
        in_specs=[SMEM] + [VMEM] * (len(operands) - 1),
        out_specs=[VMEM] * len(out_shape),
        scratch_shapes=[pltpu.VMEM(layout.state(n), jnp.float32) for n in range(1, TERMS)],
        compiler_params=pltpu.CompilerParams(vmem_limit_bytes=16 * 2**20),
        cost_estimate=cost(6 * 10**9),
        name="later_depth",
    )(*operands)


def in_upper_half(axis):
    return lax.axis_index(axis) >= lax.axis_size(axis) // 2


def all_slowness(slowness, width):
    slow = gather_rows(slowness, "freq")
    if slowness.shape[-1] == LANES:
        return slow
    upper = in_upper_half("freq")
    slow = jnp.where(upper, slow[:, ::-1], slow)
    slow = jnp.moveaxis(slow, (1, 0), (2, 3)).reshape(slowness.shape[:2] + (2, width // LANES // 2, LANES))
    slow = jnp.moveaxis(slow, (3, 2), (0, 1))
    return jnp.where(upper, slow[:, ::-1], slow)


def halves(count):
    half = count // 2
    groups = [list(range(half)), list(range(half, count))]
    return half, groups, [(i, (i + half) % count) for i in range(count)]


def sum_rows(maps, axis):
    half, groups, between = halves(lax.axis_size(axis))
    flat = maps.reshape(half, -1, maps.shape[-1])
    parts = lax.all_to_all(flat, axis, 0, 0, axis_index_groups=groups)
    summed = jnp.sum(parts, axis=0)
    summed = summed + lax.ppermute(summed, axis, between)
    spread = jnp.broadcast_to(summed[None], (half,) + summed.shape)
    return lax.all_to_all(spread, axis, 0, 0, axis_index_groups=groups).reshape(maps.shape)


def gather_rows(rows, axis):
    half, groups, between = halves(lax.axis_size(axis))
    others = lax.ppermute(rows, axis, between)
    own = lax.broadcasted_iota(jnp.int32, (half, 2) + (1,) * rows.ndim, 1) == 0
    pairs = jnp.where(own, rows, others)
    flat = pairs.reshape(half, -1, rows.shape[-1])
    return lax.all_to_all(flat, axis, 0, 0, axis_index_groups=groups).reshape(pairs.shape)


def assemble(gathered, tile_rows, width):
    half, _, steps, chunk = gathered.shape[:4]
    direct = chunk % ROWS == 0

    def body(gathered_ref, image_ref, energy_ref, staged, sems):
        copies = []

        def copy(piece, depth, start):
            out_ref, start = (image_ref, start) if start < tile_rows else (energy_ref, start - tile_rows)
            target = out_ref.at[depth, pl.ds(start, piece.shape[0])]
            copies.append(pltpu.make_async_copy(piece, target, sems.at[len(copies)]))
            copies[-1].start()

        for depth in range(steps):
            if direct:
                for p in range(half):
                    for k in range(2):
                        copy(gathered_ref.at[p, k, depth], depth, (2 * p + k) * chunk)
            else:
                for p in range(half):
                    for k in range(2):
                        start = (2 * p + k) * chunk
                        staged[depth, start : start + chunk] = gathered_ref[p, k, depth]
                for start in (0, tile_rows):
                    copy(staged.at[depth, pl.ds(start, tile_rows)], depth, start)
        for each in copies:
            each.wait()

    shape = jax.ShapeDtypeStruct((steps, tile_rows, width), jnp.float32)
    return pl.pallas_call(
        body,
        out_shape=[shape, shape],
        in_specs=[ANY if direct else VMEM],
        out_specs=[ANY] * 2,
        scratch_shapes=[
            pltpu.VMEM((steps, 2 * tile_rows, width), jnp.float32),
            pltpu.SemaphoreType.DMA((steps * 2 * half,)),
        ],
        compiler_params=pltpu.CompilerParams(vmem_limit_bytes=8 * 2**20),
        cost_estimate=cost(10**8),
        name="assemble",
    )(gathered)


def per_device(source_field, receiver_field, slowness, omegas):
    tiles = lax.axis_size("tile")
    assert tiles == 2
    swap = [(0, 1), (1, 0)]
    freqs = lax.axis_size("freq")
    tile_rows, width = source_field.shape[2], source_field.shape[3]
    scales = (1.0 / math.sqrt(omegas.shape[0] * freqs), 1.0 / (omegas.shape[0] * freqs))
    layouts = [Layout(depth, tile_rows, width) for depth in range(STEPS)]

    other_source = lax.ppermute(source_field, "tile", swap)
    other_receiver = lax.ppermute(receiver_field, "tile", swap)
    slow = all_slowness(slowness, width)
    terms = first_terms(layouts[0], source_field, receiver_field, other_source, other_receiver)
    other_slow = lax.ppermute(slow, "tile", swap)

    chunk = 2 * tile_rows // freqs
    maps, fields = first_depth(layouts[0], scales, omegas, terms, slow, other_slow)
    every = [maps]
    for depth in range(1, STEPS):
        maps, *rest = later_depth(layouts[depth], scales, omegas, fields, slow, other_slow)
        fields = rest[0] if rest else None
        every.append(maps)
    parts = jnp.stack([maps.reshape(freqs // 2, 2, chunk, width) for maps in every], 2)
    return tuple(assemble(sum_rows(parts, "freq"), tile_rows, width))


def solution(mesh):
    in_specs = (
        P("shot", "freq", "tile", None),
        P("shot", "freq", "tile", None),
        P(None, "tile", "freq"),
        P("freq"),
    )
    out_specs = (P("shot", "tile", None), P("shot", "tile", None))
    return jax.shard_map(
        per_device, mesh=mesh, in_specs=in_specs, out_specs=out_specs, check_vma=False
    )
```
